128 devices in a mesh: group: 8 (over y, core), shard: 16 (over z, x).
Axes of the slice: x: 4, y: 4, z: 4, core: 2. Of those that a mesh axis runs over, the one named last changes fastest.
Arguments:
- queries: bfloat16 [2048, 32, 128], P(('group', 'shard')), may hold values from -12 to 12
- passages: bfloat16 [8192, 64, 128], P(('group', 'shard')), may hold values from -4 to 4
- candidates: int32 [2048, 160], P(('group', 'shard')), may hold values from 0 to 8191, as said below
- passage_slot: int32 [8192], replicated, may hold values from 0 to 8191, as said below
Outputs:
- scores: float32 [2048, 160], P(('group', 'shard'))
The draws below stay inside these ranges and needn't reach their ends.
Inputs may be any that keep to these rules, and one draw needn't show every extreme that they name: `passage_slot`: every storage row is named by exactly one passage id. `candidates`: candidates k * 20 to (k + 1) * 20 - 1 of a query, for k < 8, all lie in the storage rows of one device, rows d * 64 to (d + 1) * 64 - 1 of device d counted group-major. Over the 16 queries of one device, at most 3 such groups name any one device, and some devices are named exactly 3 times by the queries of every device.
All inputs are finite; a program needn't handle non-finite values.
Results may differ from the reference program's by a relative error of at most 0.0003.
Values may be sent and summed in bfloat16 or wider, within the bound.
A program may use at most 64 MiB of HBM per device.

```python
import jax
import jax.numpy as jnp
from jax import lax

QTOK = 32
PTOK = 64
DIM = 128
PER_VISIT = 20
SPREAD = 8
Q_DEV = 16
SLOT_DEV = 64
PEERS = 128
CAND = 160
VCAP = 3
QUERIES = 2048
SLOTS = 8192


def layout(key):
    return jax.random.permutation(jax.random.fold_in(key, 11), SLOTS).astype(jnp.int32)


def entry_scales(key):
    order = jax.random.permutation(jax.random.fold_in(key, 5), DIM).astype(jnp.float32)
    return 2.0 ** (5.0 * order / (DIM - 1) - 2.5)


def draw_queries(key, part):
    scales = entry_scales(key)
    signs = jnp.where(jax.random.bernoulli(jax.random.fold_in(key, 7), 0.5, (QUERIES, QTOK, DIM)), 1.0, -1.0)
    levels = jnp.exp(jax.random.uniform(jax.random.fold_in(key, 9), (QUERIES, QTOK, 1), jnp.float32, jnp.log(0.5), jnp.log(2.0)))
    values = signs * levels / scales[None, None, :]
    return values.astype(jnp.float32).astype(jnp.bfloat16)


def draw_passages(key, part):
    scales = entry_scales(key) * DIM ** (-0.5)
    raw = jax.random.truncated_normal(jax.random.fold_in(key, 13), -3.5, 3.5, (SLOTS, PTOK, DIM), jnp.float32)
    values = raw * scales[None, None, :]
    return values.astype(jnp.float32).astype(jnp.bfloat16)


def draw_passage_slot(key, part):
    return layout(key)


def draw_candidates(key, part):
    placed = layout(key)
    inverse = jnp.zeros((SLOTS,), jnp.int32).at[placed].set(jnp.arange(SLOTS, dtype=jnp.int32))
    device_order = jax.random.permutation(jax.random.fold_in(key, 23), PEERS).astype(jnp.int32)
    device_rank = jnp.zeros((PEERS,), jnp.int32).at[device_order].set(jnp.arange(PEERS, dtype=jnp.int32))
    hot_count = PEERS // 8
    visit_count = Q_DEV * SPREAD
    cold_total = visit_count - hot_count * VCAP
    base_count = cold_total // (PEERS - hot_count)
    extra_count = cold_total % (PEERS - hot_count)
    counts = jnp.where(device_rank < hot_count, VCAP, base_count + (device_rank - hot_count < extra_count).astype(jnp.int32))
    limits = jnp.cumsum(counts.astype(jnp.int32))

    def source(source_index):
        source_key = jax.random.fold_in(key, 1000 + source_index)
        pair_index = jnp.arange(visit_count, dtype=jnp.int32)
        destination = jnp.sum((limits[None, :] <= pair_index[:, None]).astype(jnp.int32), axis=1)
        shuffle = jax.random.permutation(jax.random.fold_in(source_key, 1), visit_count)
        destination = destination[shuffle]
        local_rows = jax.random.randint(jax.random.fold_in(source_key, 2), (visit_count, PER_VISIT), 0, SLOT_DEV)
        storage = destination[:, None] * SLOT_DEV + local_rows
        return inverse[storage].reshape(Q_DEV, SPREAD * PER_VISIT)
    result = jax.vmap(source)(jnp.arange(PEERS, dtype=jnp.int32))
    return result.reshape(QUERIES, CAND).astype(jnp.int32)


def setup_inputs(seed: int = 0) -> dict:
    streams_of = jax.random.split(jax.random.key(seed), 5)
    return {
        "queries": draw_queries(jax.random.fold_in(streams_of[4], 71), 0),
        "passages": draw_passages(jax.random.fold_in(streams_of[4], 71), 0),
        "candidates": draw_candidates(jax.random.fold_in(streams_of[4], 71), 0),
        "passage_slot": draw_passage_slot(jax.random.fold_in(streams_of[4], 71), 0),
    }


def reference(queries, passages, candidates, passage_slot):
    storage = passage_slot[candidates]

    def one_query(pieces):
        query_rows, rows_wanted = pieces
        chosen = passages[rows_wanted].astype(jnp.float32)
        similarity = jnp.einsum("qd,cpd->qcp", query_rows.astype(jnp.float32), chosen)
        return jnp.sum(jnp.max(similarity, axis=2), axis=0) / QTOK

    return lax.map(one_query, (queries, storage))
```

```python
import functools

import jax
import jax.numpy as jnp
from jax import lax
from jax.experimental import pallas as pl
from jax.experimental.pallas import tpu as pltpu
from jax.sharding import PartitionSpec as P

PER_VISIT = 20
SPREAD = 8
CAP = 3
PEERS = 128
CHUNK = 16
MESH = pl.DeviceIdType.MESH


def offset_target(y, c, z, x, o, sign):
    i, j = o // 32, (o // 8) % 4
    dx, dc = (o // 2) % 4, o % 2
    dz = (j % 2) * 2 + j // 2
    dy = (i + dz + dx) % 4
    ty = (y + sign * dy + 4) % 4
    tz = (z + sign * dz + 4) % 4
    tx = (x + sign * dx + 4) % 4
    tc = (c + dc) % 2
    group, shard = ty * 2 + tc, tz * 4 + tx
    return group, shard, group * 16 + shard


def kernel(
    q_ref, p_ref, cand_ref, slot_ref, out_ref,
    send, recv, pt, p32, retsend, ret, picked, route, route_s,
    send_sem, recv_sem, retsend_sem, ret_sem, local_sem,
):
    group, shard = lax.axis_index("group"), lax.axis_index("shard")
    y, c, z, x = group // 2, group % 2, shard // 4, shard % 4
    me = group * 16 + shard
    qn, tok, dim = q_ref.shape
    rows = CAP * tok

    cand = cand_ref[...]
    wide = jnp.concatenate(
        [jnp.pad(cand[:, k * PER_VISIT:(k + 1) * PER_VISIT], ((0, 0), (0, 128 - PER_VISIT)))
         for k in range(SPREAD)], axis=0)
    cand_t = wide.T[:24]
    hi, lo = cand_t // 128, cand_t % 128
    storage = jnp.zeros((24, 128), jnp.int32)
    for h in range(64):
        line = jnp.broadcast_to(slot_ref[h:h + 1, :], (24, 128))
        storage = jnp.where(hi == h, jnp.take_along_axis(line, lo, axis=1), storage)
    local_rows = jnp.pad(storage % 64, ((0, 104), (0, 0))).T
    target = storage[0:1, :] // 64

    down = lax.broadcasted_iota(jnp.int32, (128, 128), 0)
    across = lax.broadcasted_iota(jnp.int32, (128, 128), 1)
    matches = down == target
    matches_b = jnp.where(matches, 1.0, 0.0).astype(jnp.bfloat16)
    upper = jnp.where(down < across, 1.0, 0.0).astype(jnp.bfloat16)
    before = jnp.dot(matches_b, upper, preferred_element_type=jnp.float32)
    rank = jnp.sum(jnp.where(matches, before, 0.0), axis=0, keepdims=True)
    query = (lax.broadcasted_iota(jnp.int32, (8, 128), 1) % qn).astype(jnp.float32)
    level = lax.broadcasted_iota(jnp.int32, (8, 128), 0).astype(jnp.float32)
    held = jnp.where(level == rank, query, 0.0).astype(jnp.bfloat16)
    slots = lax.dot_general(held, matches_b, (((1,), (1,)), ((), ())), preferred_element_type=jnp.float32)
    route[0:8, :] = jnp.clip(slots.astype(jnp.int32), 0, qn - 1)
    route[8:16, :] = jnp.broadcast_to(jnp.clip(target, 0, PEERS - 1), (8, 128))
    route[16:24, :] = jnp.broadcast_to(jnp.clip(rank.astype(jnp.int32), 0, CAP - 1), (8, 128))
    copy = pltpu.make_async_copy(route, route_s, local_sem)
    copy.start()
    copy.wait()

    def fill(ref, o, number):
        for r in range(CAP):
            ref[pl.ds(o * rows + r * tok, tok), :] = q_ref[route_s[r, number]]

    fill(recv, 0, me)

    @pl.loop(1, PEERS)
    def _(o):
        tg, ts, number = offset_target(y, c, z, x, o, 1)
        fill(send, o, number)
        pltpu.make_async_remote_copy(
            src_ref=send.at[pl.ds(o * rows, rows), :],
            dst_ref=recv.at[pl.ds(o * rows, rows), :],
            send_sem=send_sem,
            recv_sem=recv_sem.at[o // CHUNK],
            device_id=(tg, ts),
            device_id_type=MESH,
        ).start()

    p32[...] = p_ref[...].reshape(p32.shape).astype(jnp.float32)
    for t in range(64):
        pt[t * 64:(t + 1) * 64, :] = p32[pl.ds(t, 64, stride=64), :].astype(jnp.bfloat16)

    def score(k):
        lhs = recv[pl.ds(k * CHUNK * rows, CHUNK * rows), :]
        best = None
        for n in range(16):
            sim = lax.dot_general(
                lhs, pt[n * 256:(n + 1) * 256, :], (((1,), (1,)), ((), ())),
                preferred_element_type=jnp.float32)
            two = jnp.maximum(sim[:, :128], sim[:, 128:])
            best = two if best is None else jnp.maximum(best, two)
        best = jnp.maximum(best, pltpu.roll(best, 64, 1))
        return jnp.sum(best.reshape(CHUNK * CAP, tok, 128), axis=1) * (1.0 / tok)

    @pl.loop(0, PEERS // CHUNK)
    def _(k):
        @pl.when(k == 0)
        def _():
            part = recv.at[pl.ds(rows, (CHUNK - 1) * rows), :]
            pltpu.make_async_copy(part, part, recv_sem.at[0]).wait()

        @pl.when(k > 0)
        def _():
            part = recv.at[pl.ds(k * CHUNK * rows, CHUNK * rows), :]
            pltpu.make_async_copy(part, part, recv_sem.at[k]).wait()

        total = score(k)
        for j in range(CHUNK):
            retsend[k * CHUNK + j, 0:CAP, :] = total[j * CAP:(j + 1) * CAP, :]

        @pl.loop(0, CHUNK)
        def _(j):
            o = k * CHUNK + j

            @pl.when(o > 0)
            def _():
                tg, ts, number = offset_target(y, c, z, x, o, -1)
                pltpu.make_async_remote_copy(
                    src_ref=retsend.at[o],
                    dst_ref=ret.at[me],
                    send_sem=retsend_sem,
                    recv_sem=ret_sem,
                    device_id=(tg, ts),
                    device_id_type=MESH,
                ).start()

            @pl.when(o == 0)
            def _():
                ret[me] = retsend[0]

    part = retsend.at[pl.ds(1, PEERS - 1)]
    pltpu.make_async_copy(part, part, ret_sem).wait()

    @pl.loop(0, PEERS)
    def _(v):
        picked[pl.ds(v, 1), :] = ret[route_s[8, v], pl.ds(route_s[16, v], 1), :]

    scores = jnp.take_along_axis(picked[...], local_rows, axis=1)
    for k in range(SPREAD):
        out_ref[:, k * PER_VISIT:(k + 1) * PER_VISIT] = scores[k * qn:(k + 1) * qn, :PER_VISIT]

    pltpu.make_async_copy(part, part, retsend_sem).wait()
    part = send.at[pl.ds(rows, (PEERS - 1) * rows), :]
    pltpu.make_async_copy(part, part, send_sem).wait()


def local(queries, passages, candidates, passage_slot):
    rows = CAP * queries.shape[1]
    dim = queries.shape[2]
    return pl.pallas_call(
        kernel,
        out_shape=jax.ShapeDtypeStruct(candidates.shape, jnp.float32),
        in_specs=[pl.BlockSpec(memory_space=pltpu.VMEM)] * 4,
        out_specs=pl.BlockSpec(memory_space=pltpu.VMEM),
        scratch_shapes=[
            pltpu.VMEM((PEERS * rows, dim), jnp.bfloat16),
            pltpu.VMEM((PEERS * rows, dim), jnp.bfloat16),
            pltpu.VMEM((4096, dim), jnp.bfloat16),
            pltpu.VMEM((4096, dim), jnp.float32),
            pltpu.VMEM((PEERS, 8, 128), jnp.float32),
            pltpu.VMEM((PEERS, 8, 128), jnp.float32),
            pltpu.VMEM((PEERS, 128), jnp.float32),
            pltpu.VMEM((24, 128), jnp.int32),
            pltpu.SMEM((24, 128), jnp.int32),
            pltpu.SemaphoreType.DMA,
            pltpu.SemaphoreType.DMA((PEERS // CHUNK,)),
            pltpu.SemaphoreType.DMA,
            pltpu.SemaphoreType.DMA,
            pltpu.SemaphoreType.DMA,
        ],
        compiler_params=pltpu.CompilerParams(
            has_side_effects=True, vmem_limit_bytes=52 * 2**20),
    )(queries, passages, candidates, passage_slot.reshape(64, 128))


def solution(mesh):
    return jax.shard_map(
        local,
        mesh=mesh,
        in_specs=(
            P(("group", "shard"), None, None),
            P(("group", "shard"), None, None),
            P(("group", "shard"), None),
            P(),
        ),
        out_specs=P(("group", "shard"), None),
        check_vma=False,
    )
```

```python
import functools

import jax
import jax.numpy as jnp
from jax import lax
from jax.experimental import pallas as pl
from jax.experimental.pallas import tpu as pltpu
from jax.sharding import PartitionSpec as P

PER_VISIT = 20
SPREAD = 8
CAP = 3
PEERS = 128
CHUNK = 16
WINDOW = 8
MESH = pl.DeviceIdType.MESH


def offset_target(y, c, z, x, o, sign):
    o = (o * 27) & 127
    i, j, dx, dc = o >> 5, (o >> 3) & 3, (o >> 1) & 3, o & 1
    dz = ((j & 1) << 1) + (j >> 1)
    dy = (i + dz + dx) & 3
    ty, tz, tx, tc = (y + sign * dy) & 3, (z + sign * dz) & 3, (x + sign * dx) & 3, (c + dc) & 1
    group, shard = ty * 2 + tc, tz * 4 + tx
    return group, shard, group * 16 + shard


def kernel(
    q_hbm, p_hbm, cand_hbm, slot_hbm, out_ref,
    q_ref, p_ref, cand_ref, slot_ref, send, recv, pt, p32, retsend, ret, picked, route, route_s,
    send_sem, recv_sem, retsend_sem, ret_sem, local_sem, in_sem, ready,
):
    group, shard = lax.axis_index("group"), lax.axis_index("shard")
    y, c, z, x = group // 2, group % 2, shard // 4, shard % 4
    me = group * 16 + shard
    qn, tok, dim = q_ref.shape
    rows = CAP * tok

    inputs = [
        pltpu.make_async_copy(src, dst, in_sem.at[i])
        for i, (src, dst) in enumerate(
            ((cand_hbm, cand_ref), (slot_hbm, slot_ref), (q_hbm, q_ref), (p_hbm, p_ref)))
    ]
    for copy in inputs:
        copy.start()
    barrier = pltpu.get_barrier_semaphore()

    along_x = [(group, z * 4 + ((x + d) & 3)) for d in (1, 2, 3)]
    along_y = [(((y + d) & 3) * 2 + c, shard) for d in (1, 2, 3)]
    along_z = [(group, ((z + d) & 3) * 4 + x) for d in (1, 2, 3)]
    other = [(group + 1 - 2 * c, shard)]

    def tell(peers, sem):
        for peer in peers:
            pl.semaphore_signal(sem, inc=1, device_id=peer, device_id_type=MESH)

    tell(along_z + along_y + along_x + other, barrier)

    inputs[0].wait()
    inputs[1].wait()

    cand = cand_ref[...]
    wide = jnp.concatenate(
        [jnp.pad(cand[:, k * PER_VISIT:(k + 1) * PER_VISIT], ((0, 0), (0, 128 - PER_VISIT)))
         for k in range(SPREAD)], axis=0)
    cand_t = wide.T[:24]
    hi, lo = cand_t // 128, cand_t % 128
    storage = jnp.zeros((24, 128), jnp.int32)
    for h in range(64):
        line = jnp.broadcast_to(slot_ref[h:h + 1, :], (24, 128))
        storage = jnp.where(hi == h, jnp.take_along_axis(line, lo, axis=1), storage)
    local_rows = jnp.pad(storage % 64, ((0, 104), (0, 0))).T
    target = storage[0:1, :] // 64

    down = lax.broadcasted_iota(jnp.int32, (128, 128), 0)
    across = lax.broadcasted_iota(jnp.int32, (128, 128), 1)
    matches = down == target
    matches_b = jnp.where(matches, 1.0, 0.0).astype(jnp.bfloat16)
    upper = jnp.where(down < across, 1.0, 0.0).astype(jnp.bfloat16)
    before = jnp.dot(matches_b, upper, preferred_element_type=jnp.float32)
    rank = jnp.sum(jnp.where(matches, before, 0.0), axis=0, keepdims=True)
    query = (lax.broadcasted_iota(jnp.int32, (8, 128), 1) % qn).astype(jnp.float32)
    level = lax.broadcasted_iota(jnp.int32, (8, 128), 0).astype(jnp.float32)
    held = jnp.where(level == rank, query, 0.0).astype(jnp.bfloat16)
    slots = lax.dot_general(held, matches_b, (((1,), (1,)), ((), ())), preferred_element_type=jnp.float32)
    route[0:8, :] = jnp.clip(slots.astype(jnp.int32), 0, qn - 1)
    route[8:16, :] = jnp.broadcast_to(jnp.clip(target, 0, PEERS - 1), (8, 128))
    route[16:24, :] = jnp.broadcast_to(jnp.clip(rank.astype(jnp.int32), 0, CAP - 1), (8, 128))
    copy = pltpu.make_async_copy(route, route_s, local_sem)
    copy.start()
    copy.wait()

    def fill(ref, o, number):
        for r in range(CAP):
            ref[pl.ds(o * rows + r * tok, tok), :] = q_ref[route_s[r, number]]

    inputs[2].wait()
    fill(recv, 0, me)

    @pl.loop(1, PEERS)
    def _(o):
        _, _, number = offset_target(y, c, z, x, o, 1)
        fill(send, o, number)

    pl.semaphore_wait(barrier, 10)
    for i, peers in enumerate((along_y, along_z, other)):
        tell(peers, ready.at[i])
        pl.semaphore_wait(ready.at[i], len(peers))

    def launch(k, first):
        @pl.loop(first, CHUNK)
        def _(j):
            o = k * CHUNK + j
            tg, ts, _ = offset_target(y, c, z, x, o, 1)
            pltpu.make_async_remote_copy(
                src_ref=send.at[pl.ds(o * rows, rows), :],
                dst_ref=recv.at[pl.ds(o * rows, rows), :],
                send_sem=send_sem,
                recv_sem=recv_sem.at[k],
                device_id=(tg, ts),
                device_id_type=MESH,
            ).start()

    launch(0, 1)
    for k in range(1, WINDOW):
        launch(k, 0)

    inputs[3].wait()
    p32[...] = p_ref[...].reshape(p32.shape).astype(jnp.float32)
    for t in range(64):
        pt[t * 64:(t + 1) * 64, :] = p32[pl.ds(t, 64, stride=64), :].astype(jnp.bfloat16)

    def score(k):
        lhs = recv[pl.ds(k * CHUNK * rows, CHUNK * rows), :]
        best = None
        for n in range(16):
            sim = lax.dot_general(
                lhs, pt[n * 256:(n + 1) * 256, :], (((1,), (1,)), ((), ())),
                preferred_element_type=jnp.float32)
            two = jnp.maximum(sim[:, :128], sim[:, 128:])
            best = two if best is None else jnp.maximum(best, two)
        best = jnp.maximum(best, pltpu.roll(best, 64, 1))
        return jnp.sum(best.reshape(CHUNK * CAP, tok, 128), axis=1) * (1.0 / tok)

    @pl.loop(0, PEERS // CHUNK)
    def _(k):
        @pl.when(k == 0)
        def _():
            part = recv.at[pl.ds(rows, (CHUNK - 1) * rows), :]
            pltpu.make_async_copy(part, part, recv_sem.at[0]).wait()

        @pl.when(k > 0)
        def _():
            part = recv.at[pl.ds(k * CHUNK * rows, CHUNK * rows), :]
            pltpu.make_async_copy(part, part, recv_sem.at[k]).wait()

        @pl.when(k + WINDOW < PEERS // CHUNK)
        def _():
            launch(k + WINDOW, 0)

        total = score(k)
        for j in range(CHUNK):
            retsend[k * CHUNK + j, 0:CAP, :] = total[j * CAP:(j + 1) * CAP, :]

        @pl.loop(0, CHUNK)
        def _(j):
            o = k * CHUNK + j

            @pl.when(o > 0)
            def _():
                tg, ts, number = offset_target(y, c, z, x, o, -1)
                pltpu.make_async_remote_copy(
                    src_ref=retsend.at[o],
                    dst_ref=ret.at[me],
                    send_sem=retsend_sem,
                    recv_sem=ret_sem,
                    device_id=(tg, ts),
                    device_id_type=MESH,
                ).start()

            @pl.when(o == 0)
            def _():
                ret[me] = retsend[0]

    part = retsend.at[pl.ds(1, PEERS - 1)]
    pltpu.make_async_copy(part, part, ret_sem).wait()

    @pl.loop(0, PEERS)
    def _(v):
        picked[pl.ds(v, 1), :] = ret[route_s[8, v], pl.ds(route_s[16, v], 1), :]

    scores = jnp.take_along_axis(picked[...], local_rows, axis=1)
    for k in range(SPREAD):
        out_ref[:, k * PER_VISIT:(k + 1) * PER_VISIT] = scores[k * qn:(k + 1) * qn, :PER_VISIT]

    pltpu.make_async_copy(part, part, retsend_sem).wait()
    part = send.at[pl.ds(rows, (PEERS - 1) * rows), :]
    pltpu.make_async_copy(part, part, send_sem).wait()


def local(queries, passages, candidates, passage_slot):
    rows = CAP * queries.shape[1]
    dim = queries.shape[2]
    return pl.pallas_call(
        kernel,
        out_shape=jax.ShapeDtypeStruct(candidates.shape, jnp.float32),
        in_specs=[pl.BlockSpec(memory_space=pl.ANY)] * 4,
        out_specs=pl.BlockSpec(memory_space=pltpu.VMEM),
        scratch_shapes=[
            pltpu.VMEM(queries.shape, queries.dtype),
            pltpu.VMEM(passages.shape, passages.dtype),
            pltpu.VMEM(candidates.shape, candidates.dtype),
            pltpu.VMEM((64, 128), jnp.int32),
            pltpu.VMEM((PEERS * rows, dim), jnp.bfloat16),
            pltpu.VMEM((PEERS * rows, dim), jnp.bfloat16),
            pltpu.VMEM((4096, dim), jnp.bfloat16),
            pltpu.VMEM((4096, dim), jnp.float32),
            pltpu.VMEM((PEERS, 8, 128), jnp.float32),
            pltpu.VMEM((PEERS, 8, 128), jnp.float32),
            pltpu.VMEM((PEERS, 128), jnp.float32),
            pltpu.VMEM((24, 128), jnp.int32),
            pltpu.SMEM((24, 128), jnp.int32),
            pltpu.SemaphoreType.DMA,
            pltpu.SemaphoreType.DMA((PEERS // CHUNK,)),
            pltpu.SemaphoreType.DMA,
            pltpu.SemaphoreType.DMA,
            pltpu.SemaphoreType.DMA,
            pltpu.SemaphoreType.DMA((4,)),
            pltpu.SemaphoreType.REGULAR((3,)),
        ],
        compiler_params=pltpu.CompilerParams(
            collective_id=0, has_side_effects=True, vmem_limit_bytes=62 * 2**20),
    )(queries, passages, candidates, passage_slot.reshape(64, 128))


def solution(mesh):
    return jax.shard_map(
        local,
        mesh=mesh,
        in_specs=(
            P(("group", "shard"), None, None),
            P(("group", "shard"), None, None),
            P(("group", "shard"), None),
            P(),
        ),
        out_specs=P(("group", "shard"), None),
        check_vma=False,
    )
```

```python
import functools

import jax
import jax.numpy as jnp
from jax import lax
from jax.experimental import pallas as pl
from jax.experimental.pallas import tpu as pltpu
from jax.sharding import PartitionSpec as P

PER_VISIT = 20
SPREAD = 8
CAP = 3
PEERS = 128
CHUNK = 8
DIRECT = 24
EARLY = 2
QUEUED = 64
MESH = pl.DeviceIdType.MESH


def order():
    chips = [(0, 0, 0)]
    for d in (1, 2, 3):
        chips += [(d, 0, 0), (0, d, 0), (0, 0, d)]
    for m in range(9):
        p, q = m % 3 + 1, (m % 3 + m // 3) % 3 + 1
        chips += [(p, 0, q), (q, p, 0), (0, q, p)]
    for m in range(27):
        u, v, w = m % 3, m // 3 % 3, m // 9
        chips.append((u + 1, (u + v) % 3 + 1, (u + w) % 3 + 1))
    return [chip + (core,) for chip in chips for core in (0, 1)]


def passed_by(ahead):
    axes = [i for i in range(3) if ahead[i]]
    if len(axes) == 2:
        first = 2 if axes == [0, 2] else axes[0]
        second = sum(axes) - first
        return second if ahead[second] == 2 and ahead[first] != 2 else first
    for i in range(3):
        if ahead[i] == 2 and ahead[(i + 1) % 3] != 2:
            return i
    return sum(d == 3 for d in ahead[:3]) % 3


def kernel(
    q_hbm, p_hbm, cand_hbm, slot_hbm, out_ref,
    q_ref, p_ref, cand_ref, slot_ref, near_q, near_route, near_route_s, peer_s, send, recv, pt, p32, retsend, ret, picked, route, route_s,
    send_sem, recv_sem, retsend_sem, ret_sem, local_sem, in_sem, ready, near_sem,
):
    group, shard = lax.axis_index("group"), lax.axis_index("shard")
    y, c, z, x = group // 2, group % 2, shard // 4, shard % 4
    me = group * 16 + shard
    qn, tok, dim = q_ref.shape
    rows = CAP * tok

    inputs = [
        pltpu.make_async_copy(src, dst, in_sem.at[i])
        for i, (src, dst) in enumerate(
            ((cand_hbm, cand_ref), (slot_hbm, slot_ref), (q_hbm, q_ref), (p_hbm, p_ref)))
    ]
    for copy in inputs:
        copy.start()
    barrier = pltpu.get_barrier_semaphore()

    lines = [
        peer
        for d in (1, 2, 3)
        for peer in ((group, z * 4 + ((x + d) & 3)), (((y + d) & 3) * 2 + c, shard), (group, ((z + d) & 3) * 4 + x))
    ]
    flip = 1 - 2 * c
    chips = [(group + flip, shard)] + [(g + flip, h) for g, h in lines]

    def tell(peers, sem):
        for peer in peers:
            pl.semaphore_signal(sem, inc=1, device_id=peer, device_id_type=MESH)

    tell(lines + chips, barrier)

    inputs[0].wait()
    inputs[1].wait()

    cand = cand_ref[...]
    wide = jnp.concatenate(
        [jnp.pad(cand[:, k * PER_VISIT:(k + 1) * PER_VISIT], ((0, 0), (0, 128 - PER_VISIT)))
         for k in range(SPREAD)], axis=0)
    cand_t = wide.T[:24]
    hi, lo = cand_t // 128, cand_t % 128
    storage = jnp.zeros((24, 128), jnp.int32)
    for h in range(64):
        line = jnp.broadcast_to(slot_ref[h:h + 1, :], (24, 128))
        storage = jnp.where(hi == h, jnp.take_along_axis(line, lo, axis=1), storage)
    target = storage[0:1, :] // 64

    down = lax.broadcasted_iota(jnp.int32, (128, 128), 0)
    across = lax.broadcasted_iota(jnp.int32, (128, 128), 1)
    matches = down == target
    matches_b = jnp.where(matches, 1.0, 0.0).astype(jnp.bfloat16)
    upper = jnp.where(down < across, 1.0, 0.0).astype(jnp.bfloat16)
    before = jnp.dot(matches_b, upper, preferred_element_type=jnp.float32)
    rank = jnp.sum(jnp.where(matches, before, 0.0), axis=0, keepdims=True)
    place = storage % 64 + jnp.where(rank == 1.0, 64, 0)
    place = jnp.pad(place, ((0, 104), (0, 0))).T
    query = (lax.broadcasted_iota(jnp.int32, (8, 128), 1) % qn).astype(jnp.float32)
    level = lax.broadcasted_iota(jnp.int32, (8, 128), 0).astype(jnp.float32)
    held = jnp.where(level == rank, query, 0.0).astype(jnp.bfloat16)
    slots = lax.dot_general(held, matches_b, (((1,), (1,)), ((), ())), preferred_element_type=jnp.float32)
    route[0:8, :] = jnp.clip(slots.astype(jnp.int32), 0, qn - 1)
    route[8:16, :] = jnp.broadcast_to(jnp.clip(target, 0, PEERS - 1), (8, 128))
    route[16:24, :] = jnp.broadcast_to(jnp.where(rank > 1.0, 1, 0), (8, 128))
    copy = pltpu.make_async_copy(route, route_s, local_sem)
    copy.start()
    copy.wait()

    ahead_y = [[(((y + d) & 3) * 2 + ((c + e) & 1)) for e in (0, 1)] for d in range(4)]
    ahead_zx = [[((z + d) & 3) * 4 + ((x + e) & 3) for e in range(4)] for d in range(4)]
    for o, (dx, dy, dz, dc) in enumerate(order()):
        peer_s[0, o] = ahead_y[-dy % 4][dc]
        peer_s[1, o] = ahead_zx[-dz % 4][-dx % 4]
        if o >= DIRECT:
            axis = passed_by((dx, dy, dz))
            by = (dx, dy, dz)[axis]
            dx, dy, dz = (0 if i == axis else d for i, d in enumerate((dx, dy, dz)))
            peer_s[4, o] = axis * 3 + by - 1
        peer_s[2, o] = ahead_y[dy][dc]
        peer_s[3, o] = ahead_zx[dz][dx]

    def fill(ref, o, number):
        for r in range(CAP):
            ref[pl.ds(o * rows + r * tok, tok), :] = q_ref[route_s[r, number]]

    def fill_near(o):
        line, number = peer_s[4, o], peer_s[2, o] * 16 + peer_s[3, o]
        for r in range(CAP):
            send[pl.ds(o * rows + r * tok, tok), :] = near_q[line * qn + near_route_s[line * 8 + r, number]]

    inputs[2].wait()
    fill(recv, 0, me)

    @pl.loop(1, DIRECT)
    def _(o):
        fill(send, o, peer_s[2, o] * 16 + peer_s[3, o])

    def start(o):
        pltpu.make_async_remote_copy(
            src_ref=send.at[pl.ds(o * rows, rows), :],
            dst_ref=recv.at[pl.ds(o * rows, rows), :],
            send_sem=send_sem,
            recv_sem=recv_sem.at[o // CHUNK],
            device_id=(peer_s[2, o], peer_s[3, o]),
            device_id_type=MESH,
        ).start()

    def launch(first, end):
        @pl.loop(first, end)
        def _(o):
            start(o)

    def launch_near(first):
        for j in range(CHUNK):
            fill_near(first + j)
            start(first + j)

    pl.semaphore_wait(barrier, 19)
    tell(lines, ready.at[0])
    launch(1, 20)
    for d in (1, 2, 3):
        for axis in range(3):
            line, peer = axis * 3 + d - 1, lines[(d - 1) * 3 + axis]
            pltpu.make_async_remote_copy(
                src_ref=route.at[pl.ds(0, 8), :], dst_ref=near_route.at[pl.ds(line * 8, 8), :],
                send_sem=near_sem.at[0], recv_sem=near_sem.at[1], device_id=peer, device_id_type=MESH).start()
            pltpu.make_async_remote_copy(
                src_ref=q_ref, dst_ref=near_q.at[pl.ds(line * qn, qn)],
                send_sem=near_sem.at[2], recv_sem=near_sem.at[3], device_id=peer, device_id_type=MESH).start()
    pl.semaphore_wait(ready.at[0], 9)
    tell(lines, ready.at[1])
    launch(20, DIRECT)

    inputs[3].wait()
    p32[...] = p_ref[...].reshape(p32.shape).astype(jnp.float32)
    for t in range(64):
        pt[t * 64:(t + 1) * 64, :] = p32[pl.ds(t, 64, stride=64), :].astype(jnp.bfloat16)

    def score(k):
        lhs = recv[pl.ds(k * CHUNK * rows, CHUNK * rows), :]
        best = None
        for n in range(16):
            sim = lax.dot_general(
                lhs, pt[n * 256:(n + 1) * 256, :], (((1,), (1,)), ((), ())),
                preferred_element_type=jnp.float32)
            two = jnp.maximum(sim[:, :128], sim[:, 128:])
            best = two if best is None else jnp.maximum(best, two)
        best = jnp.maximum(best, pltpu.roll(best, 64, 1))
        return jnp.sum(best.reshape(CHUNK * CAP, tok, 128), axis=1) * (1.0 / tok)

    def step(k):
        @pl.when(k == 0)
        def _():
            part = recv.at[pl.ds(rows, (CHUNK - 1) * rows), :]
            pltpu.make_async_copy(part, part, recv_sem.at[0]).wait()

        @pl.when(k > 0)
        def _():
            part = recv.at[pl.ds(k * CHUNK * rows, CHUNK * rows), :]
            pltpu.make_async_copy(part, part, recv_sem.at[k]).wait()

        total = score(k)
        low = lax.broadcasted_iota(jnp.int32, (1, 128), 1) < 64
        for j in range(CHUNK):
            first, second, last = (total[j * CAP + r:j * CAP + r + 1, :] for r in range(CAP))
            retsend[k * CHUNK + j, 0:1, :] = jnp.where(low, first, second)
            retsend[k * CHUNK + j, 1:2, :] = last

        for j in range(CHUNK):
            o = k * CHUNK + j

            def answer():
                pltpu.make_async_remote_copy(
                    src_ref=retsend.at[o],
                    dst_ref=ret.at[me],
                    send_sem=retsend_sem,
                    recv_sem=ret_sem,
                    device_id=(peer_s[0, o], peer_s[1, o]),
                    device_id_type=MESH,
                ).start()

            if j:
                answer()
            else:
                pl.when(k > 0)(answer)

    @pl.loop(0, EARLY)
    def _(k):
        step(k)

    pltpu.make_async_copy(near_route, near_route, near_sem.at[1]).wait()
    copy = pltpu.make_async_copy(near_route, near_route_s, local_sem)
    copy.start()
    copy.wait()
    pltpu.make_async_copy(near_q, near_q, near_sem.at[3]).wait()

    @pl.loop(DIRECT // CHUNK, QUEUED // CHUNK)
    def _(i):
        launch_near(i * CHUNK)

    pl.semaphore_wait(ready.at[1], 9)

    @pl.loop(EARLY, PEERS // CHUNK)
    def _(k):
        after = k - EARLY + QUEUED // CHUNK

        @pl.when(after < PEERS // CHUNK)
        def _():
            launch_near(after * CHUNK)

        step(k)

    part = retsend.at[pl.ds(1, PEERS - 1)]
    pltpu.make_async_copy(part, part, ret_sem).wait()

    ret[me] = retsend[0]

    @pl.loop(0, PEERS, unroll=8)
    def _(v):
        picked[pl.ds(v, 1), :] = ret[route_s[8, v], pl.ds(route_s[16, v], 1), :]

    scores = jnp.take_along_axis(picked[...], place, axis=1)
    for k in range(SPREAD):
        out_ref[:, k * PER_VISIT:(k + 1) * PER_VISIT] = scores[k * qn:(k + 1) * qn, :PER_VISIT]

    pltpu.make_async_copy(part, part, retsend_sem).wait()
    pltpu.make_async_copy(near_route, near_route, near_sem.at[0]).wait()
    pltpu.make_async_copy(near_q, near_q, near_sem.at[2]).wait()
    part = send.at[pl.ds(rows, (PEERS - 1) * rows), :]
    pltpu.make_async_copy(part, part, send_sem).wait()


def local(queries, passages, candidates, passage_slot):
    rows = CAP * queries.shape[1]
    dim = queries.shape[2]
    return pl.pallas_call(
        kernel,
        out_shape=jax.ShapeDtypeStruct(candidates.shape, jnp.float32),
        in_specs=[pl.BlockSpec(memory_space=pl.ANY)] * 4,
        out_specs=pl.BlockSpec(memory_space=pltpu.VMEM),
        scratch_shapes=[
            pltpu.VMEM(queries.shape, queries.dtype),
            pltpu.VMEM(passages.shape, passages.dtype),
            pltpu.VMEM(candidates.shape, candidates.dtype),
            pltpu.VMEM((64, 128), jnp.int32),
            pltpu.VMEM((9 * queries.shape[0],) + queries.shape[1:], queries.dtype),
            pltpu.VMEM((72, 128), jnp.int32),
            pltpu.SMEM((72, 128), jnp.int32),
            pltpu.SMEM((8, 128), jnp.int32),
            pltpu.VMEM((PEERS * rows, dim), jnp.bfloat16),
            pltpu.VMEM((PEERS * rows, dim), jnp.bfloat16),
            pltpu.VMEM((4096, dim), jnp.bfloat16),
            pltpu.VMEM((4096, dim), jnp.float32),
            pltpu.VMEM((PEERS, 2, 128), jnp.float32),
            pltpu.VMEM((PEERS, 2, 128), jnp.float32),
            pltpu.VMEM((PEERS, 128), jnp.float32),
            pltpu.VMEM((24, 128), jnp.int32),
            pltpu.SMEM((24, 128), jnp.int32),
            pltpu.SemaphoreType.DMA,
            pltpu.SemaphoreType.DMA((PEERS // CHUNK,)),
            pltpu.SemaphoreType.DMA,
            pltpu.SemaphoreType.DMA,
            pltpu.SemaphoreType.DMA,
            pltpu.SemaphoreType.DMA((4,)),
            pltpu.SemaphoreType.REGULAR((2,)),
            pltpu.SemaphoreType.DMA((4,)),
        ],
        compiler_params=pltpu.CompilerParams(
            collective_id=0, has_side_effects=True, vmem_limit_bytes=62 * 2**20),
    )(queries, passages, candidates, passage_slot.reshape(64, 128))


def solution(mesh):
    return jax.shard_map(
        local,
        mesh=mesh,
        in_specs=(
            P(("group", "shard"), None, None),
            P(("group", "shard"), None, None),
            P(("group", "shard"), None),
            P(),
        ),
        out_specs=P(("group", "shard"), None),
        check_vma=False,
    )
```

```python
import functools

import jax
import jax.numpy as jnp
from jax import lax
from jax.experimental import pallas as pl
from jax.experimental.pallas import tpu as pltpu
from jax.sharding import PartitionSpec as P

PER_VISIT = 20
SPREAD = 8
CAP = 3
PEERS = 128
CHUNK = 8
DIRECT = 24
EARLY = 2
QUEUED = 64
WIDE = 1
LATE = 0
MESH = pl.DeviceIdType.MESH


def order():
    chips = [(0, 0, 0)]
    for d in (1, 2, 3):
        chips += [(d, 0, 0), (0, d, 0), (0, 0, d)]
    for m in range(9):
        p, q = m % 3 + 1, (m % 3 + m // 3) % 3 + 1
        chips += [(p, 0, q), (q, p, 0), (0, q, p)]
    far = []
    for m in range(27):
        u, v, w = m % 3, m // 3 % 3, m // 9
        far.append((u + 1, (u + v) % 3 + 1, (u + w) % 3 + 1))
    chips += sorted(far, key=lambda chip: -chip.count(2))
    return [chip + (core,) for chip in chips for core in (0, 1)]


def passed_by(ahead):
    axes = [i for i in range(3) if ahead[i]]
    if len(axes) == 2:
        first = 2 if axes == [0, 2] else axes[0]
        second = sum(axes) - first
        return second if ahead[second] == 2 and ahead[first] != 2 else first
    for i in range(3):
        if ahead[i] == 2 and ahead[(i + 1) % 3] != 2:
            return i
    return sum(d == 3 for d in ahead[:3]) % 3


def kernel(
    q_hbm, p_hbm, cand_hbm, slot_hbm, out_ref,
    q_ref, p_ref, cand_ref, slot_ref, near_q, near_route, near_route_s, peer_s, send, recv, pt, p32, retsend, ret, picked, route, route_s,
    send_sem, recv_sem, retsend_sem, ret_sem, local_sem, in_sem, ready, near_sem,
):
    group, shard = lax.axis_index("group"), lax.axis_index("shard")
    y, c, z, x = group // 2, group % 2, shard // 4, shard % 4
    me = group * 16 + shard
    qn, tok, dim = q_ref.shape
    rows = CAP * tok

    inputs = [
        pltpu.make_async_copy(src, dst, in_sem.at[i])
        for i, (src, dst) in enumerate(
            ((cand_hbm, cand_ref), (slot_hbm, slot_ref), (q_hbm, q_ref), (p_hbm, p_ref)))
    ]
    for copy in inputs:
        copy.start()
    barrier = pltpu.get_barrier_semaphore()

    lines = [
        peer
        for d in (1, 2, 3)
        for peer in ((group, z * 4 + ((x + d) & 3)), (((y + d) & 3) * 2 + c, shard), (group, ((z + d) & 3) * 4 + x))
    ]
    flip = 1 - 2 * c
    chips = [(group + flip, shard)] + [(g + flip, h) for g, h in lines]

    def tell(peers, sem):
        for peer in peers:
            pl.semaphore_signal(sem, inc=1, device_id=peer, device_id_type=MESH)

    tell(lines + chips, barrier)

    def pass_on(line, peer, queries):
        src, dst = (q_ref, near_q.at[pl.ds(line * qn, qn)]) if queries else (
            route.at[pl.ds(0, 8), :], near_route.at[pl.ds(line * 8, 8), :])
        pltpu.make_async_remote_copy(
            src_ref=src, dst_ref=dst, send_sem=near_sem.at[2 * queries], recv_sem=near_sem.at[2 * queries + 1],
            device_id=peer, device_id_type=MESH).start()

    inputs[2].wait()
    pl.semaphore_wait(barrier, 19)
    tell(lines, ready.at[0])
    inputs[0].wait()
    inputs[1].wait()

    cand = cand_ref[...]
    wide = jnp.concatenate(
        [jnp.pad(cand[:, k * PER_VISIT:(k + 1) * PER_VISIT], ((0, 0), (0, 128 - PER_VISIT)))
         for k in range(SPREAD)], axis=0)
    cand_t = wide.T[:24]
    hi, lo = cand_t // 128, cand_t % 128
    storage = jnp.zeros((24, 128), jnp.int32)
    for h in range(64):
        line = jnp.broadcast_to(slot_ref[h:h + 1, :], (24, 128))
        storage = jnp.where(hi == h, jnp.take_along_axis(line, lo, axis=1), storage)
    target = storage[0:1, :] // 64

    down = lax.broadcasted_iota(jnp.int32, (128, 128), 0)
    across = lax.broadcasted_iota(jnp.int32, (128, 128), 1)
    matches = down == target
    matches_b = jnp.where(matches, 1.0, 0.0).astype(jnp.bfloat16)
    upper = jnp.where(down < across, 1.0, 0.0).astype(jnp.bfloat16)
    before = jnp.dot(matches_b, upper, preferred_element_type=jnp.float32)
    rank = jnp.sum(jnp.where(matches, before, 0.0), axis=0, keepdims=True)
    place = storage % 64 + jnp.where(rank == 1.0, 64, 0)
    place = jnp.pad(place, ((0, 104), (0, 0))).T
    query = (lax.broadcasted_iota(jnp.int32, (8, 128), 1) % qn).astype(jnp.float32)
    level = lax.broadcasted_iota(jnp.int32, (8, 128), 0).astype(jnp.float32)
    held = jnp.where(level == rank, query, 0.0).astype(jnp.bfloat16)
    slots = lax.dot_general(held, matches_b, (((1,), (1,)), ((), ())), preferred_element_type=jnp.float32)
    route[0:8, :] = jnp.clip(slots.astype(jnp.int32), 0, qn - 1)
    route[8:16, :] = jnp.broadcast_to(jnp.clip(target, 0, PEERS - 1), (8, 128))
    route[16:24, :] = jnp.broadcast_to(jnp.where(rank > 1.0, 1, 0), (8, 128))
    copy = pltpu.make_async_copy(route, route_s, local_sem)
    copy.start()
    copy.wait()

    def fill(ref, o, number):
        for r in range(CAP):
            ref[pl.ds(o * rows + r * tok, tok), :] = q_ref[route_s[r, number]]

    ahead_y = [[(((y + d) & 3) * 2 + ((c + e) & 1)) for e in (0, 1)] for d in range(4)]
    ahead_zx = [[((z + d) & 3) * 4 + ((x + e) & 3) for e in range(4)] for d in range(4)]
    def start(o, group, shard):
        pltpu.make_async_remote_copy(
            src_ref=send.at[pl.ds(o * rows, rows), :],
            dst_ref=recv.at[pl.ds(o * rows, rows), :],
            send_sem=send_sem,
            recv_sem=recv_sem.at[o // CHUNK],
            device_id=(group, shard),
            device_id_type=MESH,
        ).start()

    def direct(first, end):
        for o, (dx, dy, dz, dc) in enumerate(order()):
            if first <= o < end:
                tg, ts = ahead_y[dy][dc], ahead_zx[dz][dx]
                fill(send, o, tg * 16 + ts)
                start(o, tg, ts)

    fill(recv, 0, me)
    direct(1, 20)
    for d in (1, 2, 3):
        for axis in range(3):
            line, peer = axis * 3 + d - 1, lines[(d - 1) * 3 + axis]
            pass_on(line, peer, 0)
            pass_on(line, peer, 1)

    def write_peers():
        for o, (dx, dy, dz, dc) in enumerate(order()):
            peer_s[0, o] = ahead_y[-dy % 4][dc]
            peer_s[1, o] = ahead_zx[-dz % 4][-dx % 4]
            if o >= DIRECT:
                axis = passed_by((dx, dy, dz))
                by = (dx, dy, dz)[axis]
                dx, dy, dz = (0 if i == axis else d for i, d in enumerate((dx, dy, dz)))
                peer_s[4, o] = axis * 3 + by - 1
            peer_s[2, o] = ahead_y[dy][dc]
            peer_s[3, o] = ahead_zx[dz][dx]

    def fill_near(o):
        line, number = peer_s[4, o], peer_s[2, o] * 16 + peer_s[3, o]
        for r in range(CAP):
            send[pl.ds(o * rows + r * tok, tok), :] = near_q[line * qn + near_route_s[line * 8 + r, number]]

    def launch_near(first):
        for j in range(CHUNK):
            fill_near(first + j)
            start(first + j, peer_s[2, first + j], peer_s[3, first + j])

    inputs[3].wait()
    p32[...] = p_ref[...].reshape(p32.shape).astype(jnp.float32)
    for t in range(64):
        pt[t * 64:(t + 1) * 64, :] = p32[pl.ds(t, 64, stride=64), :].astype(jnp.bfloat16)

    def score(first, size):
        lhs = recv[pl.ds(first * rows, size * rows), :]
        best = None
        for n in range(16):
            sim = lax.dot_general(
                lhs, pt[n * 256:(n + 1) * 256, :], (((1,), (1,)), ((), ())),
                preferred_element_type=jnp.float32)
            two = jnp.maximum(sim[:, :128], sim[:, 128:])
            best = two if best is None else jnp.maximum(best, two)
        best = jnp.maximum(best, pltpu.roll(best, 64, 1))
        return jnp.sum(best.reshape(size * CAP, tok, 128), axis=1) * (1.0 / tok)

    low = lax.broadcasted_iota(jnp.int32, (1, 128), 1) < 64

    def arrive(group, skip=0):
        part = recv.at[pl.ds((group * CHUNK + skip) * rows, (CHUNK - skip) * rows), :]
        pltpu.make_async_copy(part, part, recv_sem.at[group]).wait()

    def step(group, groups, own=False, peers=None, beside=None):
        for g in range(groups):
            arrive(group + g, 1 if own and g == 0 else 0)
        first, size = group * CHUNK, groups * CHUNK
        if beside is not None:
            beside()
        total = score(first, size)
        for j in range(size):
            one, two, three = (total[j * CAP + r:j * CAP + r + 1, :] for r in range(CAP))
            retsend[first + j, 0:1, :] = jnp.where(low, one, two)
            retsend[first + j, 1:2, :] = three
        for j in range(1 if own else 0, size):
            pltpu.make_async_remote_copy(
                src_ref=retsend.at[first + j],
                dst_ref=ret.at[me],
                send_sem=retsend_sem,
                recv_sem=ret_sem,
                device_id=peers[j] if peers else (peer_s[0, first + j], peer_s[1, first + j]),
                device_id_type=MESH,
            ).start()

    behind = [(ahead_y[-dy % 4][dc], ahead_zx[-dz % 4][-dx % 4]) for dx, dy, dz, dc in order()[:EARLY * CHUNK]]
    step(0, 1, own=True, peers=behind[:CHUNK], beside=write_peers)
    pl.semaphore_wait(ready.at[0], 9)
    tell(lines, ready.at[1])
    direct(20, DIRECT)
    for k in range(1, EARLY):
        step(k, 1, peers=behind[k * CHUNK:(k + 1) * CHUNK])

    pltpu.make_async_copy(near_route, near_route, near_sem.at[1]).wait()
    copy = pltpu.make_async_copy(near_route, near_route_s, local_sem)
    copy.start()
    copy.wait()
    pltpu.make_async_copy(near_q, near_q, near_sem.at[3]).wait()

    @pl.loop(DIRECT // CHUNK, QUEUED // CHUNK)
    def _(i):
        launch_near(i * CHUNK)

    pl.semaphore_wait(ready.at[1], 9)

    steps = (PEERS // CHUNK - EARLY - LATE) // WIDE

    @pl.loop(0, steps)
    def _(i):
        for g in range(WIDE):
            after = QUEUED // CHUNK + i * WIDE + g

            @pl.when(after < PEERS // CHUNK)
            def _():
                launch_near(after * CHUNK)

        step(EARLY + i * WIDE, WIDE)

    if LATE:
        @pl.loop(PEERS // CHUNK - LATE, PEERS // CHUNK)
        def _(i):
            step(i, 1)

    part = retsend.at[pl.ds(1, PEERS - 1)]
    pltpu.make_async_copy(part, part, ret_sem).wait()

    ret[me] = retsend[0]

    @pl.loop(0, PEERS, unroll=8)
    def _(v):
        picked[pl.ds(v, 1), :] = ret[route_s[8, v], pl.ds(route_s[16, v], 1), :]

    scores = jnp.take_along_axis(picked[...], place, axis=1)
    for k in range(SPREAD):
        out_ref[:, k * PER_VISIT:(k + 1) * PER_VISIT] = scores[k * qn:(k + 1) * qn, :PER_VISIT]

    pltpu.make_async_copy(part, part, retsend_sem).wait()
    pltpu.make_async_copy(near_route, near_route, near_sem.at[0]).wait()
    pltpu.make_async_copy(near_q, near_q, near_sem.at[2]).wait()
    part = send.at[pl.ds(rows, (PEERS - 1) * rows), :]
    pltpu.make_async_copy(part, part, send_sem).wait()


def local(queries, passages, candidates, passage_slot):
    rows = CAP * queries.shape[1]
    dim = queries.shape[2]
    return pl.pallas_call(
        kernel,
        out_shape=jax.ShapeDtypeStruct(candidates.shape, jnp.float32),
        in_specs=[pl.BlockSpec(memory_space=pl.ANY)] * 4,
        out_specs=pl.BlockSpec(memory_space=pltpu.VMEM),
        scratch_shapes=[
            pltpu.VMEM(queries.shape, queries.dtype),
            pltpu.VMEM(passages.shape, passages.dtype),
            pltpu.VMEM(candidates.shape, candidates.dtype),
            pltpu.VMEM((64, 128), jnp.int32),
            pltpu.VMEM((9 * queries.shape[0],) + queries.shape[1:], queries.dtype),
            pltpu.VMEM((72, 128), jnp.int32),
            pltpu.SMEM((72, 128), jnp.int32),
            pltpu.SMEM((8, 128), jnp.int32),
            pltpu.VMEM((PEERS * rows, dim), jnp.bfloat16),
            pltpu.VMEM((PEERS * rows, dim), jnp.bfloat16),
            pltpu.VMEM((4096, dim), jnp.bfloat16),
            pltpu.VMEM((4096, dim), jnp.float32),
            pltpu.VMEM((PEERS, 2, 128), jnp.float32),
            pltpu.VMEM((PEERS, 2, 128), jnp.float32),
            pltpu.VMEM((PEERS, 128), jnp.float32),
            pltpu.VMEM((24, 128), jnp.int32),
            pltpu.SMEM((24, 128), jnp.int32),
            pltpu.SemaphoreType.DMA,
            pltpu.SemaphoreType.DMA((PEERS // CHUNK,)),
            pltpu.SemaphoreType.DMA,
            pltpu.SemaphoreType.DMA,
            pltpu.SemaphoreType.DMA,
            pltpu.SemaphoreType.DMA((4,)),
            pltpu.SemaphoreType.REGULAR((2,)),
            pltpu.SemaphoreType.DMA((4,)),
        ],
        compiler_params=pltpu.CompilerParams(
            collective_id=0, has_side_effects=True, vmem_limit_bytes=62 * 2**20),
    )(queries, passages, candidates, passage_slot.reshape(64, 128))


def solution(mesh):
    return jax.shard_map(
        local,
        mesh=mesh,
        in_specs=(
            P(("group", "shard"), None, None),
            P(("group", "shard"), None, None),
            P(("group", "shard"), None),
            P(),
        ),
        out_specs=P(("group", "shard"), None),
        check_vma=False,
    )
```

```python
import functools

import jax
import jax.numpy as jnp
from jax import lax
from jax.experimental import pallas as pl
from jax.experimental.pallas import tpu as pltpu
from jax.sharding import PartitionSpec as P

PER_VISIT = 20
SPREAD = 8
CAP = 3
PEERS = 128
CHUNK = 8
DIRECT = 24
EARLY = 2
QUEUED = 64
WIDE = 1
LATE = 0
MESH = pl.DeviceIdType.MESH


def order():
    chips = [(0, 0, 0)]
    for d in (1, 2, 3):
        chips += [(d, 0, 0), (0, d, 0), (0, 0, d)]
    for m in range(9):
        p, q = m % 3 + 1, (m % 3 + m // 3) % 3 + 1
        chips += [(p, 0, q), (q, p, 0), (0, q, p)]
    far = []
    for m in range(27):
        u, v, w = m % 3, m // 3 % 3, m // 9
        far.append((u + 1, (u + v) % 3 + 1, (u + w) % 3 + 1))
    chips += sorted(far, key=lambda chip: -chip.count(2))
    return [chip + (core,) for chip in chips for core in (0, 1)]


def passed_by(ahead):
    axes = [i for i in range(3) if ahead[i]]
    if len(axes) == 2:
        first = 2 if axes == [0, 2] else axes[0]
        second = sum(axes) - first
        return second if ahead[second] == 2 and ahead[first] != 2 else first
    for i in range(3):
        if ahead[i] == 2 and ahead[(i + 1) % 3] != 2:
            return i
    return sum(d == 3 for d in ahead[:3]) % 3


def kernel(
    q_hbm, p_hbm, cand_hbm, slot_hbm, out_ref,
    q_ref, p_ref, cand_ref, slot_ref, near_q, near_route, near_route_s, peer_s, send, recv, pt, p32, retsend, ret, picked, route, route_s,
    send_sem, recv_sem, retsend_sem, ret_sem, local_sem, in_sem, ready, near_sem,
):
    group, shard = lax.axis_index("group"), lax.axis_index("shard")
    y, c, z, x = group // 2, group % 2, shard // 4, shard % 4
    me = group * 16 + shard
    qn, tok, dim = q_ref.shape
    rows = CAP * tok

    inputs = [
        pltpu.make_async_copy(src, dst, in_sem.at[i])
        for i, (src, dst) in enumerate(
            ((cand_hbm, cand_ref), (slot_hbm, slot_ref), (q_hbm, q_ref), (p_hbm, p_ref)))
    ]
    for copy in inputs:
        copy.start()
    barrier = pltpu.get_barrier_semaphore()

    lines = [
        peer
        for d in (1, 2, 3)
        for peer in ((group, z * 4 + ((x + d) & 3)), (((y + d) & 3) * 2 + c, shard), (group, ((z + d) & 3) * 4 + x))
    ]
    flip = 1 - 2 * c
    chips = [(group + flip, shard)] + [(g + flip, h) for g, h in lines]

    def tell(peers, sem):
        for peer in peers:
            pl.semaphore_signal(sem, inc=1, device_id=peer, device_id_type=MESH)

    tell(lines + chips, barrier)

    def pass_on(line, peer, queries):
        src, dst = (q_ref, near_q.at[pl.ds(line * qn, qn)]) if queries else (
            route.at[pl.ds(0, 8), :], near_route.at[pl.ds(line * 8, 8), :])
        pltpu.make_async_remote_copy(
            src_ref=src, dst_ref=dst, send_sem=near_sem.at[2 * queries], recv_sem=near_sem.at[2 * queries + 1],
            device_id=peer, device_id_type=MESH).start()

    inputs[2].wait()
    pl.semaphore_wait(barrier, 19)
    tell(lines, ready.at[0])
    inputs[0].wait()
    inputs[1].wait()

    cand = cand_ref[...]
    wide = jnp.concatenate(
        [jnp.pad(cand[:, k * PER_VISIT:(k + 1) * PER_VISIT], ((0, 0), (0, 128 - PER_VISIT)))
         for k in range(SPREAD)], axis=0)
    cand_t = wide.T[:24]
    hi, lo = cand_t // 128, cand_t % 128
    storage = jnp.zeros((24, 128), jnp.int32)
    for h in range(64):
        line = jnp.broadcast_to(slot_ref[h:h + 1, :], (24, 128))
        storage = jnp.where(hi == h, jnp.take_along_axis(line, lo, axis=1), storage)
    target = storage[0:1, :] // 64

    down = lax.broadcasted_iota(jnp.int32, (128, 128), 0)
    across = lax.broadcasted_iota(jnp.int32, (128, 128), 1)
    matches = down == target
    matches_b = jnp.where(matches, 1.0, 0.0).astype(jnp.bfloat16)
    upper = jnp.where(down < across, 1.0, 0.0).astype(jnp.bfloat16)
    before = jnp.dot(matches_b, upper, preferred_element_type=jnp.float32)
    rank = jnp.sum(jnp.where(matches, before, 0.0), axis=0, keepdims=True)
    place = storage % 64 + jnp.where(rank == 1.0, 64, 0)
    place = jnp.pad(place, ((0, 104), (0, 0))).T
    query = (lax.broadcasted_iota(jnp.int32, (8, 128), 1) % qn).astype(jnp.float32)
    level = lax.broadcasted_iota(jnp.int32, (8, 128), 0).astype(jnp.float32)
    held = jnp.where(level == rank, query, 0.0).astype(jnp.bfloat16)
    slots = lax.dot_general(held, matches_b, (((1,), (1,)), ((), ())), preferred_element_type=jnp.float32)
    route[0:8, :] = jnp.clip(slots.astype(jnp.int32), 0, qn - 1)
    route[8:16, :] = jnp.broadcast_to(jnp.clip(target, 0, PEERS - 1), (8, 128))
    route[16:24, :] = jnp.broadcast_to(jnp.where(rank > 1.0, 1, 0), (8, 128))
    copy = pltpu.make_async_copy(route, route_s, local_sem)
    copy.start()
    copy.wait()

    def fill(ref, o, number):
        for r in range(CAP):
            ref[pl.ds(o * rows + r * tok, tok), :] = q_ref[route_s[r, number]]

    ahead_y = [[(((y + d) & 3) * 2 + ((c + e) & 1)) for e in (0, 1)] for d in range(4)]
    ahead_zx = [[((z + d) & 3) * 4 + ((x + e) & 3) for e in range(4)] for d in range(4)]
    def start(o, group, shard):
        pltpu.make_async_remote_copy(
            src_ref=send.at[pl.ds(o * rows, rows), :],
            dst_ref=recv.at[pl.ds(o * rows, rows), :],
            send_sem=send_sem,
            recv_sem=recv_sem.at[o // CHUNK],
            device_id=(group, shard),
            device_id_type=MESH,
        ).start()

    def direct(first, end):
        for o, (dx, dy, dz, dc) in enumerate(order()):
            if first <= o < end:
                tg, ts = ahead_y[dy][dc], ahead_zx[dz][dx]
                fill(send, o, tg * 16 + ts)
                start(o, tg, ts)

    fill(recv, 0, me)
    direct(1, 20)
    for d in (1, 2, 3):
        for axis in range(3):
            line, peer = axis * 3 + d - 1, lines[(d - 1) * 3 + axis]
            pass_on(line, peer, 0)
            pass_on(line, peer, 1)

    def write_peers():
        for o, (dx, dy, dz, dc) in enumerate(order()):
            peer_s[0, o] = ahead_y[-dy % 4][dc]
            peer_s[1, o] = ahead_zx[-dz % 4][-dx % 4]
            if o >= DIRECT:
                axis = passed_by((dx, dy, dz))
                by = (dx, dy, dz)[axis]
                dx, dy, dz = (0 if i == axis else d for i, d in enumerate((dx, dy, dz)))
                peer_s[4, o] = axis * 3 + by - 1
            peer_s[2, o] = ahead_y[dy][dc]
            peer_s[3, o] = ahead_zx[dz][dx]

    def fill_near(o):
        line, number = peer_s[4, o], peer_s[2, o] * 16 + peer_s[3, o]
        for r in range(CAP):
            send[pl.ds(o * rows + r * tok, tok), :] = near_q[line * qn + near_route_s[line * 8 + r, number]]

    def launch_near(first):
        for j in range(CHUNK):
            fill_near(first + j)
            start(first + j, peer_s[2, first + j], peer_s[3, first + j])

    inputs[3].wait()
    p32[...] = p_ref[...].reshape(p32.shape).astype(jnp.float32)
    for t in range(64):
        pt[t * 64:(t + 1) * 64, :] = p32[pl.ds(t, 64, stride=64), :].astype(jnp.bfloat16)

    def score(first, size):
        lhs = recv[pl.ds(first * rows, size * rows), :]
        best = None
        for n in range(16):
            sim = lax.dot_general(
                lhs, pt[n * 256:(n + 1) * 256, :], (((1,), (1,)), ((), ())),
                preferred_element_type=jnp.float32)
            two = jnp.maximum(sim[:, :128], sim[:, 128:])
            best = two if best is None else jnp.maximum(best, two)
        best = jnp.maximum(best, pltpu.roll(best, 64, 1))
        return jnp.sum(best.reshape(size * CAP, tok, 128), axis=1) * (1.0 / tok)

    low = lax.broadcasted_iota(jnp.int32, (1, 128), 1) < 64

    def arrive(group, skip=0):
        part = recv.at[pl.ds((group * CHUNK + skip) * rows, (CHUNK - skip) * rows), :]
        pltpu.make_async_copy(part, part, recv_sem.at[group]).wait()

    def step(group, groups, own=False, peers=None, beside=None):
        for g in range(groups):
            arrive(group + g, 1 if own and g == 0 else 0)
        first, size = group * CHUNK, groups * CHUNK
        if beside is not None:
            beside()
        total = score(first, size)
        for j in range(size):
            one, two, three = (total[j * CAP + r:j * CAP + r + 1, :] for r in range(CAP))
            retsend[first + j, 0:1, :] = jnp.where(low, one, two)
            retsend[first + j, 1:2, :] = three
        for j in range(1 if own else 0, size):
            pltpu.make_async_remote_copy(
                src_ref=retsend.at[first + j],
                dst_ref=ret.at[me],
                send_sem=retsend_sem,
                recv_sem=ret_sem,
                device_id=peers[j] if peers else (peer_s[0, first + j], peer_s[1, first + j]),
                device_id_type=MESH,
            ).start()

    behind = [(ahead_y[-dy % 4][dc], ahead_zx[-dz % 4][-dx % 4]) for dx, dy, dz, dc in order()[:EARLY * CHUNK]]
    step(0, 1, own=True, peers=behind[:CHUNK], beside=write_peers)
    pl.semaphore_wait(ready.at[0], 9)
    tell(lines, ready.at[1])
    direct(20, DIRECT)
    for k in range(1, EARLY):
        step(k, 1, peers=behind[k * CHUNK:(k + 1) * CHUNK])

    pltpu.make_async_copy(near_route, near_route, near_sem.at[1]).wait()
    copy = pltpu.make_async_copy(near_route, near_route_s, local_sem)
    copy.start()
    pltpu.make_async_copy(near_q, near_q, near_sem.at[3]).wait()
    copy.wait()

    @pl.loop(DIRECT // CHUNK, QUEUED // CHUNK)
    def _(i):
        launch_near(i * CHUNK)

    pl.semaphore_wait(ready.at[1], 9)

    steps = (PEERS // CHUNK - EARLY - LATE) // WIDE

    @pl.loop(0, steps)
    def _(i):
        for g in range(WIDE):
            after = QUEUED // CHUNK + i * WIDE + g

            @pl.when(after < PEERS // CHUNK)
            def _():
                launch_near(after * CHUNK)

        step(EARLY + i * WIDE, WIDE)

    if LATE:
        @pl.loop(PEERS // CHUNK - LATE, PEERS // CHUNK)
        def _(i):
            step(i, 1)

    part = retsend.at[pl.ds(1, PEERS - 1)]
    pltpu.make_async_copy(part, part, ret_sem).wait()

    ret[me] = retsend[0]

    @pl.loop(0, PEERS, unroll=8)
    def _(v):
        picked[pl.ds(v, 1), :] = ret[route_s[8, v], pl.ds(route_s[16, v], 1), :]

    scores = jnp.take_along_axis(picked[...], place, axis=1)
    for k in range(SPREAD):
        out_ref[:, k * PER_VISIT:(k + 1) * PER_VISIT] = scores[k * qn:(k + 1) * qn, :PER_VISIT]

    pltpu.make_async_copy(part, part, retsend_sem).wait()
    pltpu.make_async_copy(near_route, near_route, near_sem.at[0]).wait()
    pltpu.make_async_copy(near_q, near_q, near_sem.at[2]).wait()
    part = send.at[pl.ds(rows, (PEERS - 1) * rows), :]
    pltpu.make_async_copy(part, part, send_sem).wait()


def local(queries, passages, candidates, passage_slot):
    rows = CAP * queries.shape[1]
    dim = queries.shape[2]
    return pl.pallas_call(
        kernel,
        out_shape=jax.ShapeDtypeStruct(candidates.shape, jnp.float32),
        in_specs=[pl.BlockSpec(memory_space=pl.ANY)] * 4,
        out_specs=pl.BlockSpec(memory_space=pltpu.VMEM),
        scratch_shapes=[
            pltpu.VMEM(queries.shape, queries.dtype),
            pltpu.VMEM(passages.shape, passages.dtype),
            pltpu.VMEM(candidates.shape, candidates.dtype),
            pltpu.VMEM((64, 128), jnp.int32),
            pltpu.VMEM((9 * queries.shape[0],) + queries.shape[1:], queries.dtype),
            pltpu.VMEM((72, 128), jnp.int32),
            pltpu.SMEM((72, 128), jnp.int32),
            pltpu.SMEM((8, 128), jnp.int32),
            pltpu.VMEM((PEERS * rows, dim), jnp.bfloat16),
            pltpu.VMEM((PEERS * rows, dim), jnp.bfloat16),
            pltpu.VMEM((4096, dim), jnp.bfloat16),
            pltpu.VMEM((4096, dim), jnp.float32),
            pltpu.VMEM((PEERS, 2, 128), jnp.float32),
            pltpu.VMEM((PEERS, 2, 128), jnp.float32),
            pltpu.VMEM((PEERS, 128), jnp.float32),
            pltpu.VMEM((24, 128), jnp.int32),
            pltpu.SMEM((24, 128), jnp.int32),
            pltpu.SemaphoreType.DMA,
            pltpu.SemaphoreType.DMA((PEERS // CHUNK,)),
            pltpu.SemaphoreType.DMA,
            pltpu.SemaphoreType.DMA,
            pltpu.SemaphoreType.DMA,
            pltpu.SemaphoreType.DMA((4,)),
            pltpu.SemaphoreType.REGULAR((2,)),
            pltpu.SemaphoreType.DMA((4,)),
        ],
        compiler_params=pltpu.CompilerParams(
            collective_id=0, has_side_effects=True, vmem_limit_bytes=62 * 2**20),
    )(queries, passages, candidates, passage_slot.reshape(64, 128))


def solution(mesh):
    return jax.shard_map(
        local,
        mesh=mesh,
        in_specs=(
            P(("group", "shard"), None, None),
            P(("group", "shard"), None, None),
            P(("group", "shard"), None),
            P(),
        ),
        out_specs=P(("group", "shard"), None),
        check_vma=False,
    )
```
